512 devices in a mesh: gx: 16 (over z), gy: 8 (over y, core), gz: 4 (over x).
Axes of the slice: x: 4, y: 4, z: 16, core: 2. Of those that a mesh axis runs over, the one named last changes fastest.
Arguments:
- right_side: float32 [4, 32, 512, 1024], P(None, 'gz', 'gx', 'gy'), may hold values from -108 to 108
- start_guess: float32 [4, 32, 512, 1024], P(None, 'gz', 'gx', 'gy'), may hold values from -6 to 6
- diagonal: float32 [32, 512, 1024], P('gz', 'gx', 'gy'), may hold values from 0.25 to 2
Outputs:
- ortho_basis: float32 [16, 32, 512, 1024], P(None, 'gz', 'gx', 'gy')
- rfactor: float32 [16, 16], replicated
The draws below stay inside these ranges and needn't reach their ends.
All inputs are finite; a program needn't handle non-finite values.
Results may differ from the reference program's by a relative error of at most 0.0003.
Values sent between devices are 32-bit elements; how exact they have to be, the bound alone decides.
A program may use at most 64 MiB of HBM per device.

```python
import jax
import jax.numpy as jnp
from jax import lax

RHS = 4
POWERS = 4
NX = 512
NY = 1024
NZ = 32


def draw_right_side(key, part):
    zpos = jnp.arange(NZ, dtype=jnp.float32) / NZ
    xpos = jnp.arange(NX, dtype=jnp.float32) / NX
    ypos = jnp.arange(NY, dtype=jnp.float32) / NY
    growth = (3.0 ** zpos)[:, None, None] * (3.0 ** xpos)[None, :, None] * (3.0 ** ypos)[None, None, :]
    shape = (RHS, NZ, NX, NY)
    base = jax.random.truncated_normal(key, -4.0, 4.0, shape, jnp.float32)
    return (base * growth[None]).astype(jnp.float32)


def block_scale(key, dims, pieces, smallest, top_value):
    def one(position, parts):
        steps = jax.random.uniform(jax.random.fold_in(jax.random.fold_in(key, 6), position), (parts,), jnp.float32, smallest / len(pieces), top_value / len(pieces))
        return jnp.repeat(jnp.exp(steps), dims[position] // parts).reshape((-1,) + (1,) * (len(dims) - position - 1))

    level = one(*pieces[0])
    for cut in pieces[1:]:
        level = level * one(*cut)
    return level


def bell_draw(key, shape, deviation, reach, pieces=(), held_as=jnp.bfloat16):
    entries = jax.random.normal(key, shape, jnp.float32) * deviation
    if len(pieces) > 0:
        entries = block_scale(key, shape, pieces, -0.22, 0.18) * entries
    return jnp.clip(entries, min=-reach, max=reach).astype(held_as)


def setup_inputs(seed: int = 0) -> dict:
    key_of = jax.random.split(jax.random.key(seed), 4)
    return {
        "right_side": draw_right_side(jax.random.fold_in(key_of[3], 71), 0),
        "start_guess": bell_draw(key_of[1], (RHS, NZ, NX, NY), 1.0, 6.0, ((1, 4), (2, 16), (3, 8)), jnp.float32),
        "diagonal": jnp.clip(0.25 + 1.75 * jax.random.uniform(key_of[2], (NZ, NX, NY), jnp.float32) ** block_scale(key_of[2], (NZ, NX, NY), ((0, 4), (1, 16), (2, 8)), -0.2, 0.2), 0.25, 2.0),
    }


shift_value = 7.125
scale_value = 3.0

def operate(field, diagonal):
    padded = jnp.pad(field, ((0, 0), (1, 1), (1, 1), (1, 1)))
    beside = padded[:, 2:, 1:-1, 1:-1] + padded[:, :-2, 1:-1, 1:-1]
    beside = beside + padded[:, 1:-1, 2:, 1:-1] + padded[:, 1:-1, :-2, 1:-1]
    beside = beside + padded[:, 1:-1, 1:-1, 2:] + padded[:, 1:-1, 1:-1, :-2]
    return (6.0 + diagonal) * field - beside

def upper_factor(gram):
    count = gram.shape[0]
    places = jnp.arange(count)
    rows = []
    for index in range(count):
        rest = gram[index]
        if index > 0:
            earlier = jnp.stack(rows, 0)
            rest = rest - jnp.dot(earlier[:, index], earlier, precision=lax.Precision.HIGHEST)
        pivot = jnp.sqrt(rest[index])
        rows.append(jnp.where(places >= index, rest / pivot, jnp.zeros_like(rest)))
    return jnp.stack(rows, 0)

def upper_inverse(upper):
    count = upper.shape[0]
    identity = jnp.eye(count, dtype=upper.dtype)
    solved = [None] * count
    for index in reversed(range(count)):
        accum = identity[index]
        if index < count - 1:
            later = jnp.stack(solved[index + 1:], 0)
            accum = accum - jnp.dot(upper[index, index + 1:], later, precision=lax.Precision.HIGHEST)
        solved[index] = accum / upper[index, index]
    return jnp.stack(solved, 0)

def reference(right_side, start_guess, diagonal):
    residual = right_side - operate(start_guess, diagonal)
    columns = [residual]
    vector = residual
    for power in range(POWERS - 1):
        vector = (operate(vector, diagonal) - shift_value * vector) / scale_value
        columns.append(vector)
    width = RHS * POWERS
    basis = jnp.concatenate(columns, 0).reshape(width, -1)
    gram = jnp.dot(basis, basis.T, precision=lax.Precision.HIGHEST)
    rfactor = upper_factor(gram)
    inverse = upper_inverse(rfactor)
    ortho = jnp.dot(inverse.T, basis, precision=lax.Precision.HIGHEST)
    return (ortho.reshape(width, NZ, NX, NY), rfactor)
```

```python
import functools

import jax
import jax.numpy as jnp
from jax import lax
from jax.experimental import pallas as pl
from jax.experimental.pallas import tpu as pltpu
from jax.sharding import PartitionSpec as P

MESH = pl.DeviceIdType.MESH
F32 = jnp.float32
RHS = 4
POWERS = 4
shift_value = 7.125
scale_value = 3.0

PAIRS = [(r, s) for r in range(RHS) for s in range(r, RHS)]
EARLY = [(k, pair) for k in range(5) for pair in PAIRS]
LATE = [(k, pair) for k in (5, 6) for pair in PAIRS]
EARLY_GROUPS = -(-len(EARLY) // 8)
LATE_GROUPS = -(-len(LATE) // 8)
GROUPS = EARLY_GROUPS + LATE_GROUPS
ROW_OF = {entry: row for row, entry in enumerate(EARLY)}
ROW_OF.update({entry: EARLY_GROUPS * 8 + row for row, entry in enumerate(LATE)})


def ring(axis, offset):
    count = lax.axis_size(axis)
    return lax.rem(lax.axis_index(axis) + (offset + count), count)


def far_first(offsets, distance):
    return sorted(offsets, key=lambda k: -distance(k))


def tree_sum(values):
    values = list(values)
    while len(values) > 1:
        values = [
            values[i] + values[i + 1] if i + 1 < len(values) else values[i]
            for i in range(0, len(values), 2)
        ]
    return values[0]


def power_kernel(
    sizes, right_hbm, guess_hbm, diag_hbm, basis_hbm, total_out,
    field, last, right, diag, y_send, y_low, y_high, x_send, x_low, x_high,
    tile0, tile1, tile2, pair_buf, plane_buf, line_buf,
    in_sem, out_sem, halo_send, halo_recv, sum_send, sum_recv,
):
    n_gx, n_gy, n_gz = sizes
    n_y = n_gy // 2
    zlen, xlen = diag.shape[0], diag.shape[1]
    xtiles = xlen // 8
    gx, gy, gz = (lax.axis_index(a) for a in ("gx", "gy", "gz"))

    load_guess = [
        pltpu.make_async_copy(guess_hbm.at[r], field.at[0, r, pl.ds(1, zlen)], in_sem.at[r])
        for r in range(RHS)
    ]
    load_rest = [
        pltpu.make_async_copy(diag_hbm, diag, in_sem.at[RHS]),
        pltpu.make_async_copy(right_hbm, right, in_sem.at[RHS + 1]),
    ]
    for copy in load_guess + load_rest:
        copy.start()

    def dist(k, n):
        return min(k, n - k)

    plane = [(dy, dx) for dy in range(n_y) for dx in range(n_gz) if (dy, dx) != (0, 0)]
    plane = far_first(plane, lambda k: dist(k[0], n_y) + dist(k[1], n_gz))
    line = far_first(range(1, n_gx), lambda k: dist(k, n_gx))

    def plane_dev(k):
        return {"gy": ring("gy", 2 * k[0]), "gz": ring("gz", k[1])}

    barrier = pltpu.get_barrier_semaphore()
    greeted = [{"gy": ring("gy", 1)}, {"gy": ring("gy", -1)}]
    greeted += [plane_dev(k) for k in reversed(plane)]
    greeted += [{"gx": ring("gx", k)} for k in reversed(line)]
    for device in greeted:
        pl.semaphore_signal(barrier, inc=1, device_id=device, device_id_type=MESH)

    lane = lax.broadcasted_iota(jnp.int32, (8, 128), 1)
    sub = lax.broadcasted_iota(jnp.int32, (8, 128), 0)
    lane_half = lane // 2
    odd = lane % 2 == 1
    first_lane, last_lane = lane == 0, lane == 127
    first_row, last_row = sub == 0, sub == 7
    y_has = [(gy > 0).astype(F32), (gy < n_gy - 1).astype(F32)]
    x_has = [(gx > 0).astype(F32), (gx < n_gx - 1).astype(F32)]
    z_has = [(gz > 0).astype(F32), (gz < n_gz - 1).astype(F32)]

    def rows(xt):
        return pl.ds(8 * xt, 8)

    def pack(packed, value, index):
        return jnp.where(lane_half == index, pltpu.roll(value, 2 * index + 1, 1), packed)

    def halo_copies(p, r):
        sends = [
            (field.at[p, r, zlen], field.at[p, r, 0], {"gz": ring("gz", 1)}),
            (field.at[p, r, 1], field.at[p, r, zlen + 1], {"gz": ring("gz", -1)}),
            (x_send.at[p, r, 1], x_low.at[p, r], {"gx": ring("gx", 1)}),
            (x_send.at[p, r, 0], x_high.at[p, r], {"gx": ring("gx", -1)}),
            (y_send.at[p, r], y_low.at[p, r], {"gy": ring("gy", 1)}),
            (y_send.at[p, r], y_high.at[p, r], {"gy": ring("gy", -1)}),
        ]
        return [
            pltpu.make_async_remote_copy(
                src_ref=src, dst_ref=dst, send_sem=halo_send.at[p, r, i],
                recv_sem=halo_recv.at[p, r, i], device_id=device, device_id_type=MESH,
            )
            for i, (src, dst, device) in enumerate(sends)
        ]

    def keep_x_faces(p, r, z, xt, value):
        if xt == 0:
            x_send[p, r, 0, z : z + 1, :] = value[0:1, :]
        if xt == xtiles - 1:
            x_send[p, r, 1, z : z + 1, :] = value[7:8, :]

    for r in range(RHS):
        load_guess[r].wait()
        packed = jnp.zeros((8, 128), F32)
        for z in range(zlen):
            for xt in range(xtiles):
                value = field[0, r, z + 1, rows(xt), :]
                packed = pack(packed, value, z * xtiles + xt)
                keep_x_faces(0, r, z, xt, value)
        y_send[0, r] = packed
        if r == 0:
            pl.semaphore_wait(barrier, len(greeted))
        for copy in halo_copies(0, r):
            copy.start()
    for copy in load_rest:
        copy.wait()

    def step(p, r):
        for copy in halo_copies(p, r):
            copy.wait_recv()
        edges = jnp.where(
            odd, pltpu.roll(y_high[p, r] * y_has[1], 126, 1), y_low[p, r] * y_has[0]
        )
        x_lo = x_low[p, r] * x_has[0]
        x_hi = x_high[p, r] * x_has[1]
        packed = jnp.zeros((8, 128), F32)
        for z in range(zlen):
            for xt in range(xtiles):
                index = z * xtiles + xt
                here = field[p, r, z + 1, rows(xt), :]
                z_lo = field[p, r, z, rows(xt), :]
                z_hi = field[p, r, z + 2, rows(xt), :]
                if z == 0:
                    z_lo = z_lo * z_has[0]
                if z == zlen - 1:
                    z_hi = z_hi * z_has[1]
                if xt == 0:
                    below = jnp.where(first_row, x_lo[z : z + 1, :], pltpu.roll(here, 1, 0))
                else:
                    below = field[p, r, z + 1, pl.ds(8 * xt - 1, 8), :]
                if xt == xtiles - 1:
                    above = jnp.where(last_row, x_hi[z : z + 1, :], pltpu.roll(here, 7, 0))
                else:
                    above = field[p, r, z + 1, pl.ds(8 * xt + 1, 8), :]
                edge = edges if index == 0 else pltpu.roll(edges, 128 - 2 * index, 1)
                left = jnp.where(first_lane, edge, pltpu.roll(here, 1, 1))
                far = jnp.where(last_lane, edge, pltpu.roll(here, 127, 1))
                beside = ((z_lo + z_hi) + (below + above)) + (left + far)
                weight = diag[z, rows(xt), :]
                if p == 0:
                    value = right[r, z, rows(xt), :] - ((6.0 + weight) * here - beside)
                else:
                    value = ((weight + (6.0 - shift_value)) * here - beside) * (1.0 / scale_value)
                if p < POWERS - 1:
                    field[p + 1, r, z + 1, rows(xt), :] = value
                    packed = pack(packed, value, index)
                    keep_x_faces(p + 1, r, z, xt, value)
                else:
                    last[r, z, rows(xt), :] = value
        if p < POWERS - 1:
            y_send[p + 1, r] = packed
            for copy in halo_copies(p + 1, r):
                copy.start()

    def vector(p, r, z, xt):
        if p < POWERS - 1:
            return field[p + 1, r, z + 1, rows(xt), :]
        return last[r, z, rows(xt), :]

    def moments(p):
        n = len(PAIRS) * (1 if p == 0 else 2)

        def body(z, sums):
            sums = list(sums)
            for xt in range(xtiles):
                now = [vector(p, r, z, xt) for r in range(RHS)]
                products = []
                if p > 0:
                    before = [vector(p - 1, r, z, xt) for r in range(RHS)]
                    products += [before[r] * now[s] for r, s in PAIRS]
                products += [now[r] * now[s] for r, s in PAIRS]
                sums = [a + b for a, b in zip(sums, products, strict=True)]
            return tuple(sums)

        return list(lax.fori_loop(0, zlen, body, (jnp.zeros((8, 128), F32),) * n))

    def fold(sums, first_group):
        tile = jnp.zeros((8, 128), F32)
        for g in range(0, len(sums), 8):
            some = [jnp.sum(s, axis=0, keepdims=True) for s in sums[g : g + 8]]
            some += [jnp.zeros((1, 128), F32)] * (8 - len(some))
            sums_of = jnp.sum(jnp.concatenate(some, 0), axis=1, keepdims=True)
            tile = jnp.where(lane == first_group + g // 8, sums_of, tile)
        return tile

    out_copies = []
    early = []
    for p in range(POWERS):
        lax.fori_loop(0, RHS, lambda r, c, p=p: (step(p, r), c)[1], 0)
        if p < POWERS - 1:
            early += moments(p)
        else:
            late = moments(p)
        for r in range(RHS):
            src = field.at[p + 1, r, pl.ds(1, zlen)] if p < POWERS - 1 else last.at[r]
            copy = pltpu.make_async_copy(src, basis_hbm.at[p * RHS + r], out_sem.at[p * RHS + r])
            copy.start()
            out_copies.append(copy)
        if p == POWERS - 2:
            tile0[...] = fold(early, 0)

    tile0[...] += fold(late, EARLY_GROUPS)

    sends = []

    def exchange(src, dst, number, device):
        copy = pltpu.make_async_remote_copy(
            src_ref=src, dst_ref=dst, send_sem=sum_send.at[number],
            recv_sem=sum_recv.at[number], device_id=device, device_id_type=MESH,
        )
        copy.start()
        sends.append(copy)
        return copy

    mate = {"gy": gy + 1 - 2 * lax.rem(gy, 2)}
    exchange(tile0, pair_buf, 0, mate).wait_recv()
    tile1[...] = tile0[...] + pair_buf[...]

    slot = (gy // 2) * n_gz + gz
    copies = [
        exchange(tile1, plane_buf.at[slot], 1 + i, plane_dev(k)) for i, k in enumerate(plane)
    ]
    plane_buf[slot] = tile1[...]
    for copy in copies:
        copy.wait_recv()
    tile2[...] = tree_sum([plane_buf[i] for i in range(n_y * n_gz)])

    base = n_y * n_gz
    copies = [
        exchange(tile2, line_buf.at[gx], base + i, {"gx": ring("gx", k)})
        for i, k in enumerate(line)
    ]
    line_buf[gx] = tile2[...]
    for copy in copies:
        copy.wait_recv()
    total_out[...] = tree_sum([line_buf[i] for i in range(n_gx)])

    for copy in sends:
        copy.wait_send()
    for p in range(POWERS):
        for r in range(RHS):
            for copy in halo_copies(p, r):
                copy.wait_send()
    for copy in out_copies:
        copy.wait()


def factor_kernel(total, basis_hbm, ortho_hbm, factor, table, coeff, block, result, in_sem, out_sem):
    width = RHS * POWERS
    zlen, xlen = block.shape[1], block.shape[2]
    loads = [
        pltpu.make_async_copy(basis_hbm.at[:, z], block.at[:, z], in_sem.at[z]) for z in range(zlen)
    ]
    for copy in loads:
        copy.start()
    whole = total[...]
    for g in range(GROUPS):
        table[8 * g : 8 * g + 8, :] = jnp.broadcast_to(whole[:, g : g + 1], (8, 128))

    def gram(i, j):
        r, s = sorted((i % RHS, j % RHS))
        row = ROW_OF[(i // RHS + j // RHS, (r, s))]
        return jnp.broadcast_to(table[row : row + 1, :], (8, 128))

    lane = lax.broadcasted_iota(jnp.int32, (1, 128), 1)
    upper = {}
    for k in range(width):
        rest = {}
        for j in range(k, width):
            value = gram(k, j)
            for i in range(k):
                value = value - upper[i, k] * upper[i, j]
            rest[j] = value
        pivot = rest[k]
        inverse = lax.rsqrt(pivot)
        inverse = inverse * (1.5 - 0.5 * pivot * inverse * inverse)
        row = jnp.zeros((1, 128), F32)
        for j in range(k, width):
            upper[k, j] = rest[j] * inverse
            row = jnp.where(lane == j, upper[k, j][0:1, :], row)
            coeff[k * width + j] = inverse if j == k else upper[k, j]
        factor[k : k + 1, :] = row[:, :width]

    def body(z, carry):
        for xt in range(0, xlen // 8, 2):
            cols = [
                [block[j, z, pl.ds(8 * (xt + h), 8), :] for j in range(width)] for h in range(2)
            ]
            for i in range(width):
                scale = coeff[i * width + i]
                for h in range(2):
                    cols[h][i] = cols[h][i] * scale
                    result[i, z, pl.ds(8 * (xt + h), 8), :] = cols[h][i]
                for j in range(i + 1, width):
                    weight = coeff[i * width + j]
                    for h in range(2):
                        cols[h][j] = cols[h][j] - weight * cols[h][i]
        pltpu.make_async_copy(result.at[:, z], ortho_hbm.at[:, z], out_sem.at[z]).start()
        return carry

    for copy in loads:
        copy.wait()
    lax.fori_loop(0, zlen, body, 0)
    for z in range(zlen):
        pltpu.make_async_copy(result.at[:, z], ortho_hbm.at[:, z], out_sem.at[z]).wait()


def local(sizes, right_side, start_guess, diagonal):
    zlen, xlen, ylen = diagonal.shape
    width = RHS * POWERS
    block = (width, zlen, xlen, ylen)
    any_spec = pl.BlockSpec(memory_space=pl.ANY)
    vmem_spec = pl.BlockSpec(memory_space=pltpu.VMEM)
    n_gx, n_gy, n_gz = sizes
    planes = (n_gy // 2) * n_gz
    n_sum = planes + n_gx
    face = (POWERS, RHS, 8, 128)
    tile = pltpu.VMEM((8, 128), F32)
    basis, total = pl.pallas_call(
        functools.partial(power_kernel, sizes),
        out_shape=(jax.ShapeDtypeStruct(block, F32), jax.ShapeDtypeStruct((8, 128), F32)),
        in_specs=[any_spec] * 3,
        out_specs=(any_spec, vmem_spec),
        scratch_shapes=[
            pltpu.VMEM((POWERS, RHS, zlen + 2, xlen, ylen), F32),
            pltpu.VMEM((RHS, zlen, xlen, ylen), F32),
            pltpu.VMEM((RHS, zlen, xlen, ylen), F32),
            pltpu.VMEM((zlen, xlen, ylen), F32),
            pltpu.VMEM(face, F32),
            pltpu.VMEM(face, F32),
            pltpu.VMEM(face, F32),
            pltpu.VMEM((POWERS, RHS, 2, 8, 128), F32),
            pltpu.VMEM(face, F32),
            pltpu.VMEM(face, F32),
            tile,
            tile,
            tile,
            tile,
            pltpu.VMEM((planes, 8, 128), F32),
            pltpu.VMEM((n_gx, 8, 128), F32),
            pltpu.SemaphoreType.DMA((RHS + 2,)),
            pltpu.SemaphoreType.DMA((width,)),
            pltpu.SemaphoreType.DMA((POWERS, RHS, 6)),
            pltpu.SemaphoreType.DMA((POWERS, RHS, 6)),
            pltpu.SemaphoreType.DMA((n_sum,)),
            pltpu.SemaphoreType.DMA((n_sum,)),
        ],
        compiler_params=pltpu.CompilerParams(
            collective_id=0, has_side_effects=True, vmem_limit_bytes=24 << 20
        ),
    )(right_side, start_guess, diagonal)
    return pl.pallas_call(
        factor_kernel,
        out_shape=(
            jax.ShapeDtypeStruct(block, F32),
            jax.ShapeDtypeStruct((width, width), F32),
        ),
        in_specs=[vmem_spec, any_spec],
        out_specs=(any_spec, vmem_spec),
        scratch_shapes=[
            pltpu.VMEM((8 * GROUPS, 128), F32),
            pltpu.VMEM((width * width, 8, 128), F32),
            pltpu.VMEM(block, F32),
            pltpu.VMEM(block, F32),
            pltpu.SemaphoreType.DMA((zlen,)),
            pltpu.SemaphoreType.DMA((zlen,)),
        ],
        compiler_params=pltpu.CompilerParams(vmem_limit_bytes=24 << 20),
    )(total, basis)


def solution(mesh):
    placed = (P(None, "gz", "gx", "gy"), P(None, "gz", "gx", "gy"), P("gz", "gx", "gy"))
    sizes = tuple(mesh.shape[a] for a in ("gx", "gy", "gz"))
    return jax.shard_map(
        functools.partial(local, sizes),
        mesh=mesh,
        in_specs=placed,
        out_specs=(P(None, "gz", "gx", "gy"), P()),
        check_vma=False,
    )
```

```python
import functools

import jax
import jax.numpy as jnp
from jax import lax
from jax.experimental import pallas as pl
from jax.experimental.pallas import tpu as pltpu
from jax.sharding import PartitionSpec as P

MESH = pl.DeviceIdType.MESH
F32 = jnp.float32
RHS = 4
POWERS = 4
shift_value = 7.125
scale_value = 3.0

PAIRS = [(r, s) for r in range(RHS) for s in range(r, RHS)]
EARLY = [(k, pair) for k in range(5) for pair in PAIRS]
LATE = [(k, pair) for k in (5, 6) for pair in PAIRS]
EARLY_GROUPS = -(-len(EARLY) // 8)
LATE_GROUPS = -(-len(LATE) // 8)
GROUPS = EARLY_GROUPS + LATE_GROUPS
ROW_OF = {entry: row for row, entry in enumerate(EARLY)}
ROW_OF.update({entry: EARLY_GROUPS * 8 + row for row, entry in enumerate(LATE)})


def ring(axis, offset):
    count = lax.axis_size(axis)
    return lax.rem(lax.axis_index(axis) + (offset + count), count)


def far_first(offsets, distance):
    return sorted(offsets, key=lambda k: -distance(k))


def tree_sum(values):
    values = list(values)
    while len(values) > 1:
        values = [
            values[i] + values[i + 1] if i + 1 < len(values) else values[i]
            for i in range(0, len(values), 2)
        ]
    return values[0]


def power_kernel(
    sizes, right_hbm, guess_hbm, diag_hbm, basis, total_out,
    guess, right, diag, z_low, z_high, y_send, y_low, y_high, x_send, x_low, x_high,
    tile0, tile1, tile2, pair_buf, plane_buf, line_buf,
    in_sem, halo_send, halo_recv, sum_send, sum_recv, relay_near, relay_far,
):
    n_gx, n_gy, n_gz = sizes
    n_y = n_gy // 2
    zlen, xlen = diag.shape[0], diag.shape[1]
    xtiles = xlen // 8
    gx, gy, gz = (lax.axis_index(a) for a in ("gx", "gy", "gz"))

    load_guess = [
        pltpu.make_async_copy(guess_hbm.at[r], guess.at[r], in_sem.at[r])
        for r in range(RHS)
    ]
    load_rest = [
        pltpu.make_async_copy(diag_hbm, diag, in_sem.at[RHS]),
        pltpu.make_async_copy(right_hbm, right, in_sem.at[RHS + 1]),
    ]
    for copy in load_guess + load_rest:
        copy.start()

    def dist(k, n):
        return min(k, n - k)

    plane = [(dy, dx) for dy in range(n_y) for dx in range(n_gz) if (dy, dx) != (0, 0)]
    plane = far_first(plane, lambda k: dist(k[0], n_y) + dist(k[1], n_gz))
    line = far_first(range(1, n_gx), lambda k: dist(k, n_gx))

    def plane_dev(k):
        return {"gy": ring("gy", 2 * k[0]), "gz": ring("gz", k[1])}

    barrier = pltpu.get_barrier_semaphore()
    greeted = [{a: ring(a, k)} for a in ("gz", "gx", "gy") for k in (1, -1)]
    for device in greeted:
        pl.semaphore_signal(barrier, inc=1, device_id=device, device_id_type=MESH)

    lane = lax.broadcasted_iota(jnp.int32, (8, 128), 1)
    sub = lax.broadcasted_iota(jnp.int32, (8, 128), 0)
    lane_half = lane // 2
    odd = lane % 2 == 1
    first_lane, last_lane = lane == 0, lane == 127
    first_row, last_row = sub == 0, sub == 7
    y_has = [(gy > 0).astype(F32), (gy < n_gy - 1).astype(F32)]
    x_has = [(gx > 0).astype(F32), (gx < n_gx - 1).astype(F32)]
    z_has = [(gz > 0).astype(F32), (gz < n_gz - 1).astype(F32)]

    def rows(xt):
        return pl.ds(8 * xt, 8)

    def source(p, r):
        return (guess, r) if p == 0 else (basis, (p - 1) * RHS + r)

    def pack(packed, value, index):
        return jnp.where(lane_half == index, pltpu.roll(value, 2 * index + 1, 1), packed)

    def halo_copies(p, r):
        ref, slot = source(p, r)
        sends = [
            (ref.at[slot, zlen - 1], z_low.at[p, r], {"gz": ring("gz", 1)}),
            (ref.at[slot, 0], z_high.at[p, r], {"gz": ring("gz", -1)}),
            (x_send.at[p, r, 1], x_low.at[p, r], {"gx": ring("gx", 1)}),
            (x_send.at[p, r, 0], x_high.at[p, r], {"gx": ring("gx", -1)}),
            (y_send.at[p, r], y_low.at[p, r], {"gy": ring("gy", 1)}),
            (y_send.at[p, r], y_high.at[p, r], {"gy": ring("gy", -1)}),
        ]
        return [
            pltpu.make_async_remote_copy(
                src_ref=src, dst_ref=dst, send_sem=halo_send.at[p, r, i],
                recv_sem=halo_recv.at[p, r, i], device_id=device, device_id_type=MESH,
            )
            for i, (src, dst, device) in enumerate(sends)
        ]

    def keep_x_faces(p, r, z, xt, value):
        if xt == 0:
            x_send[p, r, 0, z : z + 1, :] = value[0:1, :]
        if xt == xtiles - 1:
            x_send[p, r, 1, z : z + 1, :] = value[7:8, :]

    for r in range(RHS):
        load_guess[r].wait()
        packed = jnp.zeros((8, 128), F32)
        for z in range(zlen):
            for xt in range(xtiles):
                value = guess[r, z, rows(xt), :]
                packed = pack(packed, value, z * xtiles + xt)
                keep_x_faces(0, r, z, xt, value)
        y_send[0, r] = packed
        if r == 0:
            pl.semaphore_wait(barrier, len(greeted))
        for copy in halo_copies(0, r):
            copy.start()
    for copy in load_rest:
        copy.wait()

    def step(p, r):
        ref, slot = source(p, r)
        for copy in halo_copies(p, r):
            copy.wait_recv()
        edges = jnp.where(
            odd, pltpu.roll(y_high[p, r] * y_has[1], 126, 1), y_low[p, r] * y_has[0]
        )
        x_lo = x_low[p, r] * x_has[0]
        x_hi = x_high[p, r] * x_has[1]
        packed = jnp.zeros((8, 128), F32)
        for z in range(zlen):
            for xt in range(xtiles):
                index = z * xtiles + xt
                here = ref[slot, z, rows(xt), :]
                if z == 0:
                    z_lo = z_low[p, r, rows(xt), :] * z_has[0]
                else:
                    z_lo = ref[slot, z - 1, rows(xt), :]
                if z == zlen - 1:
                    z_hi = z_high[p, r, rows(xt), :] * z_has[1]
                else:
                    z_hi = ref[slot, z + 1, rows(xt), :]
                if xt == 0:
                    below = jnp.where(first_row, x_lo[z : z + 1, :], pltpu.roll(here, 1, 0))
                else:
                    below = ref[slot, z, pl.ds(8 * xt - 1, 8), :]
                if xt == xtiles - 1:
                    above = jnp.where(last_row, x_hi[z : z + 1, :], pltpu.roll(here, 7, 0))
                else:
                    above = ref[slot, z, pl.ds(8 * xt + 1, 8), :]
                edge = edges if index == 0 else pltpu.roll(edges, 128 - 2 * index, 1)
                left = jnp.where(first_lane, edge, pltpu.roll(here, 1, 1))
                far = jnp.where(last_lane, edge, pltpu.roll(here, 127, 1))
                beside = ((z_lo + z_hi) + (below + above)) + (left + far)
                weight = diag[z, rows(xt), :]
                if p == 0:
                    value = right[r, z, rows(xt), :] - ((6.0 + weight) * here - beside)
                else:
                    value = ((weight + (6.0 - shift_value)) * here - beside) * (1.0 / scale_value)
                basis[p * RHS + r, z, rows(xt), :] = value
                if p < POWERS - 1:
                    packed = pack(packed, value, index)
                    keep_x_faces(p + 1, r, z, xt, value)
        if p < POWERS - 1:
            y_send[p + 1, r] = packed
            for copy in halo_copies(p + 1, r):
                copy.start()

    def vector(p, r, z, xt):
        return basis[p * RHS + r, z, rows(xt), :]

    def moments(p):
        n = len(PAIRS) * (1 if p == 0 else 2)

        def body(z, sums):
            sums = list(sums)
            for xt in range(xtiles):
                now = [vector(p, r, z, xt) for r in range(RHS)]
                products = []
                if p > 0:
                    before = [vector(p - 1, r, z, xt) for r in range(RHS)]
                    products += [before[r] * now[s] for r, s in PAIRS]
                products += [now[r] * now[s] for r, s in PAIRS]
                sums = [a + b for a, b in zip(sums, products, strict=True)]
            return tuple(sums)

        return list(lax.fori_loop(0, zlen, body, (jnp.zeros((8, 128), F32),) * n))

    def fold(sums, first_group):
        tile = jnp.zeros((8, 128), F32)
        for g in range(0, len(sums), 8):
            some = [jnp.sum(s, axis=0, keepdims=True) for s in sums[g : g + 8]]
            some += [jnp.zeros((1, 128), F32)] * (8 - len(some))
            sums_of = jnp.sum(jnp.concatenate(some, 0), axis=1, keepdims=True)
            tile = jnp.where(lane == first_group + g // 8, sums_of, tile)
        return tile

    relayed = n_gx == 16 and n_gy == 8

    def relay(sem, offsets):
        if relayed:
            for axis, k in offsets:
                pl.semaphore_signal(sem, inc=1, device_id={axis: ring(axis, k)}, device_id_type=MESH)

    near = [(axis, k) for axis in ("gx", "gy") for k in (2, -2)]
    far = [("gx", k) for k in (4, -4)]

    early = []
    for p in range(POWERS):
        step(p, 0)
        if p == 0:
            relay(relay_near, near)
        if p == 1 and relayed:
            pl.semaphore_wait(relay_near, len(near))
            relay(relay_far, far)
        if p == POWERS - 1 and relayed:
            pl.semaphore_wait(relay_far, len(far))
        lax.fori_loop(1, RHS, lambda r, c, p=p: (step(p, r), c)[1], 0)
        if p < POWERS - 1:
            early += moments(p)
        else:
            late = moments(p)
        if p == POWERS - 2:
            tile0[...] = fold(early, 0)

    tile0[...] += fold(late, EARLY_GROUPS)

    sends = []

    def exchange(src, dst, number, device):
        copy = pltpu.make_async_remote_copy(
            src_ref=src, dst_ref=dst, send_sem=sum_send.at[number],
            recv_sem=sum_recv.at[number], device_id=device, device_id_type=MESH,
        )
        copy.start()
        sends.append(copy)
        return copy

    mate = {"gy": gy + 1 - 2 * lax.rem(gy, 2)}
    exchange(tile0, pair_buf, 0, mate).wait_recv()
    tile1[...] = tile0[...] + pair_buf[...]

    slot = (gy // 2) * n_gz + gz
    copies = [
        exchange(tile1, plane_buf.at[slot], 1 + i, plane_dev(k)) for i, k in enumerate(plane)
    ]
    plane_buf[slot] = tile1[...]
    for copy in copies:
        copy.wait_recv()
    tile2[...] = tree_sum([plane_buf[i] for i in range(n_y * n_gz)])

    base = n_y * n_gz
    copies = [
        exchange(tile2, line_buf.at[gx], base + i, {"gx": ring("gx", k)})
        for i, k in enumerate(line)
    ]
    line_buf[gx] = tile2[...]
    for copy in copies:
        copy.wait_recv()
    total_out[...] = tree_sum([line_buf[i] for i in range(n_gx)])

    for copy in sends:
        copy.wait_send()
    for p in range(POWERS):
        for r in range(RHS):
            for copy in halo_copies(p, r):
                copy.wait_send()


def factor_kernel(total, basis, ortho_hbm, factor, table, coeff, result, out_sem):
    width = RHS * POWERS
    zlen, xlen = basis.shape[1], basis.shape[2]
    whole = total[...]
    for g in range(GROUPS):
        table[8 * g : 8 * g + 8, :] = jnp.broadcast_to(whole[:, g : g + 1], (8, 128))

    def gram(i, j):
        r, s = sorted((i % RHS, j % RHS))
        row = ROW_OF[(i // RHS + j // RHS, (r, s))]
        return jnp.broadcast_to(table[row : row + 1, :], (8, 128))

    lane = lax.broadcasted_iota(jnp.int32, (1, 128), 1)
    upper = {}
    for k in range(width):
        rest = {}
        for j in range(k, width):
            value = gram(k, j)
            for i in range(k):
                value = value - upper[i, k] * upper[i, j]
            rest[j] = value
        pivot = rest[k]
        inverse = lax.rsqrt(pivot)
        inverse = inverse * (1.5 - 0.5 * pivot * inverse * inverse)
        row = jnp.zeros((1, 128), F32)
        for j in range(k, width):
            upper[k, j] = rest[j] * inverse
            row = jnp.where(lane == j, upper[k, j][0:1, :], row)
            coeff[k * width + j] = inverse if j == k else upper[k, j]
        factor[k : k + 1, :] = row[:, :width]

    def body(z, carry):
        for xt in range(0, xlen // 8, 2):
            cols = [
                [basis[j, z, pl.ds(8 * (xt + h), 8), :] for j in range(width)] for h in range(2)
            ]
            for i in range(width):
                scale = coeff[i * width + i]
                for h in range(2):
                    cols[h][i] = cols[h][i] * scale
                    result[i, z, pl.ds(8 * (xt + h), 8), :] = cols[h][i]
                for j in range(i + 1, width):
                    weight = coeff[i * width + j]
                    for h in range(2):
                        cols[h][j] = cols[h][j] - weight * cols[h][i]
        pltpu.make_async_copy(result.at[:, z], ortho_hbm.at[:, z], out_sem.at[z]).start()
        return carry

    lax.fori_loop(0, zlen, body, 0)
    for z in range(zlen):
        pltpu.make_async_copy(result.at[:, z], ortho_hbm.at[:, z], out_sem.at[z]).wait()


def local(sizes, right_side, start_guess, diagonal):
    zlen, xlen, ylen = diagonal.shape
    width = RHS * POWERS
    block = (width, zlen, xlen, ylen)
    any_spec = pl.BlockSpec(memory_space=pl.ANY)
    vmem_spec = pl.BlockSpec(memory_space=pltpu.VMEM)
    n_gx, n_gy, n_gz = sizes
    planes = (n_gy // 2) * n_gz
    n_sum = planes + n_gx
    face = (POWERS, RHS, 8, 128)
    tile = pltpu.VMEM((8, 128), F32)
    basis, total = pl.pallas_call(
        functools.partial(power_kernel, sizes),
        out_shape=(jax.ShapeDtypeStruct(block, F32), jax.ShapeDtypeStruct((8, 128), F32)),
        in_specs=[any_spec] * 3,
        out_specs=(vmem_spec, vmem_spec),
        scratch_shapes=[
            pltpu.VMEM((RHS, zlen, xlen, ylen), F32),
            pltpu.VMEM((RHS, zlen, xlen, ylen), F32),
            pltpu.VMEM((zlen, xlen, ylen), F32),
            pltpu.VMEM((POWERS, RHS, xlen, ylen), F32),
            pltpu.VMEM((POWERS, RHS, xlen, ylen), F32),
            pltpu.VMEM(face, F32),
            pltpu.VMEM(face, F32),
            pltpu.VMEM(face, F32),
            pltpu.VMEM((POWERS, RHS, 2, 8, 128), F32),
            pltpu.VMEM(face, F32),
            pltpu.VMEM(face, F32),
            tile,
            tile,
            tile,
            tile,
            pltpu.VMEM((planes, 8, 128), F32),
            pltpu.VMEM((n_gx, 8, 128), F32),
            pltpu.SemaphoreType.DMA((RHS + 2,)),
            pltpu.SemaphoreType.DMA((POWERS, RHS, 6)),
            pltpu.SemaphoreType.DMA((POWERS, RHS, 6)),
            pltpu.SemaphoreType.DMA((n_sum,)),
            pltpu.SemaphoreType.DMA((n_sum,)),
            pltpu.SemaphoreType.REGULAR,
            pltpu.SemaphoreType.REGULAR,
        ],
        compiler_params=pltpu.CompilerParams(
            collective_id=0, has_side_effects=True, vmem_limit_bytes=24 << 20
        ),
    )(*[pltpu.with_memory_space_constraint(x, pltpu.HBM) for x in (right_side, start_guess, diagonal)])
    return pl.pallas_call(
        factor_kernel,
        out_shape=(
            jax.ShapeDtypeStruct(block, F32),
            jax.ShapeDtypeStruct((width, width), F32),
        ),
        in_specs=[vmem_spec, vmem_spec],
        out_specs=(any_spec, vmem_spec),
        scratch_shapes=[
            pltpu.VMEM((8 * GROUPS, 128), F32),
            pltpu.VMEM((width * width, 8, 128), F32),
            pltpu.VMEM(block, F32),
            pltpu.SemaphoreType.DMA((zlen,)),
        ],
        compiler_params=pltpu.CompilerParams(vmem_limit_bytes=24 << 20),
    )(total, basis)


def solution(mesh):
    placed = (P(None, "gz", "gx", "gy"), P(None, "gz", "gx", "gy"), P("gz", "gx", "gy"))
    sizes = tuple(mesh.shape[a] for a in ("gx", "gy", "gz"))
    return jax.shard_map(
        functools.partial(local, sizes),
        mesh=mesh,
        in_specs=placed,
        out_specs=(P(None, "gz", "gx", "gy"), P()),
        check_vma=False,
    )
```

```python
import functools

import jax
import jax.numpy as jnp
from jax import lax
from jax.experimental import pallas as pl
from jax.experimental.pallas import tpu as pltpu
from jax.sharding import PartitionSpec as P

MESH = pl.DeviceIdType.MESH
F32 = jnp.float32
RHS = 4
POWERS = 4
shift_value = 7.125
scale_value = 3.0

PAIRS = [(r, s) for r in range(RHS) for s in range(r, RHS)]
EARLY = [(k, pair) for k in range(5) for pair in PAIRS]
LATE = [(k, pair) for k in (5, 6) for pair in PAIRS]
EARLY_GROUPS = -(-len(EARLY) // 8)
LATE_GROUPS = -(-len(LATE) // 8)
GROUPS = EARLY_GROUPS + LATE_GROUPS
ROW_OF = {entry: row for row, entry in enumerate(EARLY)}
ROW_OF.update({entry: EARLY_GROUPS * 8 + row for row, entry in enumerate(LATE)})


def ring(axis, offset):
    count = lax.axis_size(axis)
    return lax.rem(lax.axis_index(axis) + (offset + count), count)


def far_first(offsets, distance):
    return sorted(offsets, key=lambda k: -distance(k))


def tree_sum(values):
    values = list(values)
    while len(values) > 1:
        values = [
            values[i] + values[i + 1] if i + 1 < len(values) else values[i]
            for i in range(0, len(values), 2)
        ]
    return values[0]


def power_kernel(
    sizes, right_hbm, guess_hbm, diag_hbm, basis, total_out,
    guess, right, diag, z_low, z_high, y_send, y_low, y_high, x_send, x_low, x_high,
    tile0, tile1, tile2, pair_buf, plane_buf, line_buf, count_ref,
    in_sem, halo_send, halo_recv, sum_send, sum_recv, relay_near, relay_far,
):
    n_gx, n_gy, n_gz = sizes
    n_y = n_gy // 2
    zlen, xlen = diag.shape[0], diag.shape[1]
    xtiles = xlen // 8
    gx, gy, gz = (lax.axis_index(a) for a in ("gx", "gy", "gz"))

    load_guess = [
        pltpu.make_async_copy(guess_hbm.at[r], guess.at[r], in_sem.at[r])
        for r in range(RHS)
    ]
    load_rest = [
        pltpu.make_async_copy(diag_hbm, diag, in_sem.at[RHS]),
        pltpu.make_async_copy(right_hbm, right, in_sem.at[RHS + 1]),
    ]
    for copy in load_guess + load_rest:
        copy.start()

    def dist(k, n):
        return min(k, n - k)

    plane = [(dy, dx) for dy in range(n_y) for dx in range(n_gz) if (dy, dx) != (0, 0)]
    plane = far_first(plane, lambda k: dist(k[0], n_y) + dist(k[1], n_gz))
    line = far_first(range(1, n_gx), lambda k: dist(k, n_gx))

    def plane_dev(k):
        return {"gy": ring("gy", 2 * k[0]), "gz": ring("gz", k[1])}

    barrier = pltpu.get_barrier_semaphore()
    greeted = [{a: ring(a, k)} for a in ("gz", "gx", "gy") for k in (1, -1)]
    for device in greeted:
        pl.semaphore_signal(barrier, inc=1, device_id=device, device_id_type=MESH)

    lane = lax.broadcasted_iota(jnp.int32, (8, 128), 1)
    sub = lax.broadcasted_iota(jnp.int32, (8, 128), 0)
    lane_half = lane // 2
    odd = lane % 2 == 1
    first_lane, last_lane = lane == 0, lane == 127
    first_row, last_row = sub == 0, sub == 7
    y_has = [(gy > 0).astype(F32), (gy < n_gy - 1).astype(F32)]
    x_has = [(gx > 0).astype(F32), (gx < n_gx - 1).astype(F32)]
    z_has = [(gz > 0).astype(F32), (gz < n_gz - 1).astype(F32)]

    def rows(xt):
        return pl.ds(8 * xt, 8)

    def source(p, r):
        return (guess, r) if p == 0 else (basis, (p - 1) * RHS + r)

    def pack(packed, value, index):
        return jnp.where(lane_half == index, pltpu.roll(value, 2 * index + 1, 1), packed)

    def send_halos(p, r, part):
        ref, slot = source(p, r)
        sends = [
            (ref.at[slot, zlen - 1], z_low.at[p, r], {"gz": ring("gz", 1)}),
            (ref.at[slot, 0], z_high.at[p, r], {"gz": ring("gz", -1)}),
            (x_send.at[p, r, 1], x_low.at[p, r], {"gx": ring("gx", 1)}),
            (x_send.at[p, r, 0], x_high.at[p, r], {"gx": ring("gx", -1)}),
            (y_send.at[p, r], y_low.at[p, r], {"gy": ring("gy", 1)}),
            (y_send.at[p, r], y_high.at[p, r], {"gy": ring("gy", -1)}),
        ]
        for src, dst, device in sends[part]:
            pltpu.make_async_remote_copy(
                src_ref=src, dst_ref=dst, send_sem=halo_send.at[p],
                recv_sem=halo_recv.at[p, r], device_id=device, device_id_type=MESH,
            ).start()

    def wait_bytes(like, sem):
        pltpu.make_async_copy(like, like, sem).wait()

    def wait_halos(p, r):
        wait_bytes(right_hbm.at[0, pl.ds(0, 3)], halo_recv.at[p, r])

    def keep_x_faces(p, r, z, xt, value):
        if xt == 0:
            x_send[p, r, 0, z : z + 1, :] = value[0:1, :]
        if xt == xtiles - 1:
            x_send[p, r, 1, z : z + 1, :] = value[7:8, :]

    for r in range(RHS):
        load_guess[r].wait()
        packed = jnp.zeros((8, 128), F32)
        for z in range(zlen):
            for xt in range(xtiles):
                value = guess[r, z, rows(xt), :]
                packed = pack(packed, value, z * xtiles + xt)
                keep_x_faces(0, r, z, xt, value)
        y_send[0, r] = packed
        if r == 0:
            pl.semaphore_wait(barrier, len(greeted))
        send_halos(0, r, slice(0, 6))
    for copy in load_rest:
        copy.wait()

    def step(p, r):
        ref, slot = source(p, r)
        wait_halos(p, r)
        edges = jnp.where(
            odd, pltpu.roll(y_high[p, r] * y_has[1], 126, 1), y_low[p, r] * y_has[0]
        )
        x_lo = x_low[p, r] * x_has[0]
        x_hi = x_high[p, r] * x_has[1]
        packed = jnp.zeros((8, 128), F32)
        for z in [0, zlen - 1, *range(1, zlen - 1)]:
            if p < POWERS - 1 and z == 1:
                send_halos(p + 1, r, slice(0, 2))
            for xt in range(xtiles):
                index = z * xtiles + xt
                here = ref[slot, z, rows(xt), :]
                if z == 0:
                    z_lo = z_low[p, r, rows(xt), :] * z_has[0]
                else:
                    z_lo = ref[slot, z - 1, rows(xt), :]
                if z == zlen - 1:
                    z_hi = z_high[p, r, rows(xt), :] * z_has[1]
                else:
                    z_hi = ref[slot, z + 1, rows(xt), :]
                if xt == 0:
                    below = jnp.where(first_row, x_lo[z : z + 1, :], pltpu.roll(here, 1, 0))
                else:
                    below = ref[slot, z, pl.ds(8 * xt - 1, 8), :]
                if xt == xtiles - 1:
                    above = jnp.where(last_row, x_hi[z : z + 1, :], pltpu.roll(here, 7, 0))
                else:
                    above = ref[slot, z, pl.ds(8 * xt + 1, 8), :]
                edge = edges if index == 0 else pltpu.roll(edges, 128 - 2 * index, 1)
                left = jnp.where(first_lane, edge, pltpu.roll(here, 1, 1))
                far = jnp.where(last_lane, edge, pltpu.roll(here, 127, 1))
                beside = ((z_lo + z_hi) + (below + above)) + (left + far)
                weight = diag[z, rows(xt), :]
                if p == 0:
                    value = right[r, z, rows(xt), :] - ((6.0 + weight) * here - beside)
                else:
                    value = ((weight + (6.0 - shift_value)) * here - beside) * (1.0 / scale_value)
                basis[p * RHS + r, z, rows(xt), :] = value
                if p < POWERS - 1:
                    packed = pack(packed, value, index)
                    keep_x_faces(p + 1, r, z, xt, value)
        if p < POWERS - 1:
            y_send[p + 1, r] = packed
            send_halos(p + 1, r, slice(2, 6))

    def vector(p, r, z, xt):
        return basis[p * RHS + r, z, rows(xt), :]

    def moments(p):
        n = len(PAIRS) * (1 if p == 0 else 2)

        def body(z, sums):
            sums = list(sums)
            for xt in range(xtiles):
                now = [vector(p, r, z, xt) for r in range(RHS)]
                products = []
                if p > 0:
                    before = [vector(p - 1, r, z, xt) for r in range(RHS)]
                    products += [before[r] * now[s] for r, s in PAIRS]
                products += [now[r] * now[s] for r, s in PAIRS]
                sums = [a + b for a, b in zip(sums, products, strict=True)]
            return tuple(sums)

        return list(lax.fori_loop(0, zlen, body, (jnp.zeros((8, 128), F32),) * n))

    def fold(sums, first_group):
        tile = jnp.zeros((8, 128), F32)
        for g in range(0, len(sums), 8):
            some = [jnp.sum(s, axis=0, keepdims=True) for s in sums[g : g + 8]]
            some += [jnp.zeros((1, 128), F32)] * (8 - len(some))
            sums_of = jnp.sum(jnp.concatenate(some, 0), axis=1, keepdims=True)
            tile = jnp.where(lane == 8 * first_group + g + sub, sums_of, tile)
        return jnp.sum(tile, axis=0, keepdims=True)

    relayed = n_gx == 16 and n_gy == 8

    def relay(sem, offsets):
        if relayed:
            for axis, k in offsets:
                pl.semaphore_signal(sem, inc=1, device_id={axis: ring(axis, k)}, device_id_type=MESH)

    near = [(axis, k) for axis in ("gx", "gy") for k in (2, -2)]
    far = [("gx", k) for k in (4, -4)]

    early = []
    for p in range(POWERS):
        step(p, 0)
        if p == 0:
            relay(relay_near, near)
        if p == 1 and relayed:
            pl.semaphore_wait(relay_near, len(near))
            relay(relay_far, far)
        if p == POWERS - 1 and relayed:
            pl.semaphore_wait(relay_far, len(far))
        lax.fori_loop(1, RHS, lambda r, c, p=p: (step(p, r), c)[1], 0)
        if p < POWERS - 1:
            early += moments(p)
        else:
            late = moments(p)
        if p == POWERS - 2:
            tile0[...] = fold(early, 0)

    tile0[...] += fold(late, EARLY_GROUPS)

    def exchange(src, dst, phase, device):
        pltpu.make_async_remote_copy(
            src_ref=src, dst_ref=dst, send_sem=sum_send.at[phase],
            recv_sem=sum_recv.at[phase], device_id=device, device_id_type=MESH,
        ).start()

    def wait_sums(sems, phase, number):
        wait_bytes(count_ref.at[pl.ds(0, number)], sems.at[phase])

    n_plane = n_y * n_gz
    slot = (gy // 2) * n_gz + gz

    exchange(tile0, pair_buf, 0, {"gy": gy + 1 - 2 * lax.rem(gy, 2)})
    wait_sums(sum_recv, 0, 1)
    tile1[...] = tile0[...] + pair_buf[...]

    for k in plane:
        exchange(tile1, plane_buf.at[slot], 1, plane_dev(k))
    plane_buf[slot] = tile1[...]
    for p in range(POWERS):
        wait_bytes(right_hbm.at[:, pl.ds(0, 3)], halo_send.at[p])
    wait_sums(sum_send, 0, 1)
    wait_sums(sum_recv, 1, n_plane - 1)
    tile2[...] = tree_sum([plane_buf[i] for i in range(n_plane)])

    for k in line:
        exchange(tile2, line_buf.at[gx], 2, {"gx": ring("gx", k)})
    line_buf[gx] = tile2[...]
    wait_sums(sum_send, 1, n_plane - 1)
    wait_sums(sum_recv, 2, n_gx - 1)
    total_out[...] = tree_sum([line_buf[i] for i in range(n_gx)])
    wait_sums(sum_send, 2, n_gx - 1)


def factor_kernel(total, basis, ortho_hbm, factor, table, coeff, result, out_sem):
    width = RHS * POWERS
    zlen, xlen = basis.shape[1], basis.shape[2]
    whole = total[...]
    places = lax.broadcasted_iota(jnp.int32, (8, 128), 1) - lax.broadcasted_iota(
        jnp.int32, (8, 128), 0
    )
    for g in range(GROUPS):
        column = jnp.sum(jnp.where(places == 8 * g, whole, 0.0), axis=1, keepdims=True)
        table[8 * g : 8 * g + 8, :] = jnp.broadcast_to(column, (8, 128))

    def gram(i, j):
        r, s = sorted((i % RHS, j % RHS))
        row = ROW_OF[(i // RHS + j // RHS, (r, s))]
        return jnp.broadcast_to(table[row : row + 1, :], (8, 128))

    lane = lax.broadcasted_iota(jnp.int32, (1, 128), 1)
    upper = {}
    for k in range(width):
        rest = {}
        for j in range(k, width):
            value = gram(k, j)
            for i in range(k):
                value = value - upper[i, k] * upper[i, j]
            rest[j] = value
        pivot = rest[k]
        inverse = lax.rsqrt(pivot)
        inverse = inverse * (1.5 - 0.5 * pivot * inverse * inverse)
        row = jnp.zeros((1, 128), F32)
        for j in range(k, width):
            upper[k, j] = rest[j] * inverse
            row = jnp.where(lane == j, upper[k, j][0:1, :], row)
            coeff[k * width + j] = inverse if j == k else upper[k, j]
        factor[k : k + 1, :] = row[:, :width]

    def body(z, carry):
        for xt in range(0, xlen // 8, 2):
            cols = [
                [basis[j, z, pl.ds(8 * (xt + h), 8), :] for j in range(width)] for h in range(2)
            ]
            for i in range(width):
                scale = coeff[i * width + i]
                for h in range(2):
                    cols[h][i] = cols[h][i] * scale
                    result[i, z, pl.ds(8 * (xt + h), 8), :] = cols[h][i]
                for j in range(i + 1, width):
                    weight = coeff[i * width + j]
                    for h in range(2):
                        cols[h][j] = cols[h][j] - weight * cols[h][i]
        pltpu.make_async_copy(result.at[:, z], ortho_hbm.at[:, z], out_sem.at[z]).start()
        return carry

    lax.fori_loop(0, zlen, body, 0)
    for z in range(zlen):
        pltpu.make_async_copy(result.at[:, z], ortho_hbm.at[:, z], out_sem.at[z]).wait()


def local(sizes, right_side, start_guess, diagonal):
    zlen, xlen, ylen = diagonal.shape
    width = RHS * POWERS
    block = (width, zlen, xlen, ylen)
    any_spec = pl.BlockSpec(memory_space=pl.ANY)
    vmem_spec = pl.BlockSpec(memory_space=pltpu.VMEM)
    n_gx, n_gy, n_gz = sizes
    planes = (n_gy // 2) * n_gz
    face = (POWERS, RHS, 8, 128)
    tile = pltpu.VMEM((1, 128), F32)
    basis, total = pl.pallas_call(
        functools.partial(power_kernel, sizes),
        out_shape=(jax.ShapeDtypeStruct(block, F32), jax.ShapeDtypeStruct((1, 128), F32)),
        in_specs=[any_spec] * 3,
        out_specs=(vmem_spec, vmem_spec),
        scratch_shapes=[
            pltpu.VMEM((RHS, zlen, xlen, ylen), F32),
            pltpu.VMEM((RHS, zlen, xlen, ylen), F32),
            pltpu.VMEM((zlen, xlen, ylen), F32),
            pltpu.VMEM((POWERS, RHS, xlen, ylen), F32),
            pltpu.VMEM((POWERS, RHS, xlen, ylen), F32),
            pltpu.VMEM(face, F32),
            pltpu.VMEM(face, F32),
            pltpu.VMEM(face, F32),
            pltpu.VMEM((POWERS, RHS, 2, 8, 128), F32),
            pltpu.VMEM(face, F32),
            pltpu.VMEM(face, F32),
            tile,
            tile,
            tile,
            tile,
            pltpu.VMEM((planes, 1, 128), F32),
            pltpu.VMEM((n_gx, 1, 128), F32),
            pltpu.VMEM((max(planes, n_gx), 1, 128), F32),
            pltpu.SemaphoreType.DMA((RHS + 2,)),
            pltpu.SemaphoreType.DMA((POWERS,)),
            pltpu.SemaphoreType.DMA((POWERS, RHS)),
            pltpu.SemaphoreType.DMA((3,)),
            pltpu.SemaphoreType.DMA((3,)),
            pltpu.SemaphoreType.REGULAR,
            pltpu.SemaphoreType.REGULAR,
        ],
        compiler_params=pltpu.CompilerParams(
            collective_id=0, has_side_effects=True, vmem_limit_bytes=24 << 20
        ),
    )(*[pltpu.with_memory_space_constraint(x, pltpu.HBM) for x in (right_side, start_guess, diagonal)])
    return pl.pallas_call(
        factor_kernel,
        out_shape=(
            jax.ShapeDtypeStruct(block, F32),
            jax.ShapeDtypeStruct((width, width), F32),
        ),
        in_specs=[vmem_spec, vmem_spec],
        out_specs=(any_spec, vmem_spec),
        scratch_shapes=[
            pltpu.VMEM((8 * GROUPS, 128), F32),
            pltpu.VMEM((width * width, 8, 128), F32),
            pltpu.VMEM(block, F32),
            pltpu.SemaphoreType.DMA((zlen,)),
        ],
        compiler_params=pltpu.CompilerParams(vmem_limit_bytes=24 << 20),
    )(total, basis)


def solution(mesh):
    placed = (P(None, "gz", "gx", "gy"), P(None, "gz", "gx", "gy"), P("gz", "gx", "gy"))
    sizes = tuple(mesh.shape[a] for a in ("gx", "gy", "gz"))
    return jax.shard_map(
        functools.partial(local, sizes),
        mesh=mesh,
        in_specs=placed,
        out_specs=(P(None, "gz", "gx", "gy"), P()),
        check_vma=False,
    )
```

```python
import functools

import jax
import jax.numpy as jnp
from jax import lax
from jax.experimental import pallas as pl
from jax.experimental.pallas import tpu as pltpu
from jax.sharding import PartitionSpec as P

MESH = pl.DeviceIdType.MESH
F32 = jnp.float32
RHS = 4
POWERS = 4
shift_value = 7.125
scale_value = 3.0

PAIRS = [(r, s) for r in range(RHS) for s in range(r, RHS)]
EARLY = [(k, pair) for k in range(5) for pair in PAIRS]
LATE = [[(k, (r, s)) for k in (5, 6) for r in range(s + 1)] for s in range(RHS)]
BATCHES = [EARLY, sum(LATE[:-1], []), LATE[-1]]
FIRST_GROUP = [0]
for entries in BATCHES:
    FIRST_GROUP.append(FIRST_GROUP[-1] - (-len(entries) // 8))
GROUPS = FIRST_GROUP[-1]
ROW_OF = {
    entry: 8 * first + row
    for first, entries in zip(FIRST_GROUP, BATCHES)
    for row, entry in enumerate(entries)
}


def ring(axis, offset):
    count = lax.axis_size(axis)
    return lax.rem(lax.axis_index(axis) + (offset + count), count)


def far_first(offsets, distance):
    return sorted(offsets, key=lambda k: -distance(k))


def tree_sum(values):
    values = list(values)
    while len(values) > 1:
        values = [
            values[i] + values[i + 1] if i + 1 < len(values) else values[i]
            for i in range(0, len(values), 2)
        ]
    return values[0]


def power_kernel(
    sizes, right_hbm, guess_hbm, diag_hbm, basis, total_out,
    guess, right, diag, z_low, z_high, y_send, y_low, y_high, x_send, x_low, x_high,
    tile0, tile1, tile2, pair_buf, plane_buf, line_buf, count_ref,
    in_sem, halo_send, halo_recv, sum_send, sum_recv, relay_near, relay_far,
):
    n_gx, n_gy, n_gz = sizes
    n_y = n_gy // 2
    zlen, xlen = diag.shape[0], diag.shape[1]
    xtiles = xlen // 8
    gx, gy, gz = (lax.axis_index(a) for a in ("gx", "gy", "gz"))

    load_guess = [
        pltpu.make_async_copy(guess_hbm.at[r], guess.at[r], in_sem.at[r]) for r in range(RHS)
    ]
    load_rest = [
        pltpu.make_async_copy(diag_hbm, diag, in_sem.at[RHS]),
        pltpu.make_async_copy(right_hbm, right, in_sem.at[RHS + 1]),
    ]
    load_guess[0].start()

    def dist(k, n):
        return min(k, n - k)

    plane = [(dy, dx) for dy in range(n_y) for dx in range(n_gz) if (dy, dx) != (0, 0)]
    plane = far_first(plane, lambda k: dist(k[0], n_y) + dist(k[1], n_gz))
    line = far_first(range(1, n_gx), lambda k: dist(k, n_gx))

    def plane_dev(k):
        return {"gy": ring("gy", 2 * k[0]), "gz": ring("gz", k[1])}

    barrier = pltpu.get_barrier_semaphore()
    greeted = [{a: ring(a, k)} for a in ("gz", "gx", "gy") for k in (1, -1)]
    for device in greeted:
        pl.semaphore_signal(barrier, inc=1, device_id=device, device_id_type=MESH)

    for copy in load_guess[1:] + load_rest:
        copy.start()

    lane = lax.broadcasted_iota(jnp.int32, (8, 128), 1)
    sub = lax.broadcasted_iota(jnp.int32, (8, 128), 0)
    lane_half = lane // 2
    odd = lane % 2 == 1
    first_lane, last_lane = lane == 0, lane == 127
    first_row, last_row = sub == 0, sub == 7
    y_has = [(gy > 0).astype(F32), (gy < n_gy - 1).astype(F32)]
    x_has = [(gx > 0).astype(F32), (gx < n_gx - 1).astype(F32)]
    z_has = [(gz > 0).astype(F32), (gz < n_gz - 1).astype(F32)]

    def rows(xt):
        return pl.ds(8 * xt, 8)

    def source(p, r):
        return (guess, r) if p == 0 else (basis, (p - 1) * RHS + r)

    def pack(packed, value, index):
        return jnp.where(lane_half == index, pltpu.roll(value, 2 * index + 1, 1), packed)

    def send_halos(p, r, part):
        ref, slot = source(p, r)
        sends = [
            (ref.at[slot, zlen - 1], z_low.at[p, r], {"gz": ring("gz", 1)}),
            (ref.at[slot, 0], z_high.at[p, r], {"gz": ring("gz", -1)}),
            (x_send.at[p, r, 1], x_low.at[p, r], {"gx": ring("gx", 1)}),
            (x_send.at[p, r, 0], x_high.at[p, r], {"gx": ring("gx", -1)}),
            (y_send.at[p, r], y_low.at[p, r], {"gy": ring("gy", 1)}),
            (y_send.at[p, r], y_high.at[p, r], {"gy": ring("gy", -1)}),
        ]
        for src, dst, device in sends[part]:
            pltpu.make_async_remote_copy(
                src_ref=src, dst_ref=dst, send_sem=halo_send.at[p],
                recv_sem=halo_recv.at[p, r], device_id=device, device_id_type=MESH,
            ).start()

    def wait_bytes(like, sem):
        pltpu.make_async_copy(like, like, sem).wait()

    def wait_halos(p, r):
        wait_bytes(right_hbm.at[0, pl.ds(0, 3)], halo_recv.at[p, r])

    def keep_x_faces(p, r, z, xt, value):
        if xt == 0:
            x_send[p, r, 0, z : z + 1, :] = value[0:1, :]
        if xt == xtiles - 1:
            x_send[p, r, 1, z : z + 1, :] = value[7:8, :]

    for r in range(RHS):
        load_guess[r].wait()
        packed = jnp.zeros((8, 128), F32)
        for z in range(zlen):
            for xt in range(xtiles):
                value = guess[r, z, rows(xt), :]
                packed = pack(packed, value, z * xtiles + xt)
                keep_x_faces(0, r, z, xt, value)
        y_send[0, r] = packed
        if r == 0:
            pl.semaphore_wait(barrier, len(greeted))
        send_halos(0, r, slice(0, 6))
    for copy in load_rest:
        copy.wait()

    def step(p, r):
        ref, slot = source(p, r)
        sums = [jnp.zeros((8, 128), F32)] * (2 * (r + 1) if p == POWERS - 1 else 0)
        wait_halos(p, r)
        edges = jnp.where(
            odd, pltpu.roll(y_high[p, r] * y_has[1], 126, 1), y_low[p, r] * y_has[0]
        )
        x_lo = x_low[p, r] * x_has[0]
        x_hi = x_high[p, r] * x_has[1]
        packed = jnp.zeros((8, 128), F32)
        for z in [0, zlen - 1, *range(1, zlen - 1)]:
            if p < POWERS - 1 and z == 1:
                send_halos(p + 1, r, slice(0, 2))
            for xt in range(xtiles):
                index = z * xtiles + xt
                here = ref[slot, z, rows(xt), :]
                if z == 0:
                    z_lo = z_low[p, r, rows(xt), :] * z_has[0]
                else:
                    z_lo = ref[slot, z - 1, rows(xt), :]
                if z == zlen - 1:
                    z_hi = z_high[p, r, rows(xt), :] * z_has[1]
                else:
                    z_hi = ref[slot, z + 1, rows(xt), :]
                if xt == 0:
                    below = jnp.where(first_row, x_lo[z : z + 1, :], pltpu.roll(here, 1, 0))
                else:
                    below = ref[slot, z, pl.ds(8 * xt - 1, 8), :]
                if xt == xtiles - 1:
                    above = jnp.where(last_row, x_hi[z : z + 1, :], pltpu.roll(here, 7, 0))
                else:
                    above = ref[slot, z, pl.ds(8 * xt + 1, 8), :]
                edge = edges if index == 0 else pltpu.roll(edges, 128 - 2 * index, 1)
                left = jnp.where(first_lane, edge, pltpu.roll(here, 1, 1))
                far = jnp.where(last_lane, edge, pltpu.roll(here, 127, 1))
                beside = ((z_lo + z_hi) + (below + above)) + (left + far)
                weight = diag[z, rows(xt), :]
                if p == 0:
                    value = right[r, z, rows(xt), :] - ((6.0 + weight) * here - beside)
                else:
                    value = ((weight + (6.0 - shift_value)) * here - beside) * (1.0 / scale_value)
                basis[p * RHS + r, z, rows(xt), :] = value
                if p == POWERS - 1:
                    others = [basis[(p - 1) * RHS + q, z, rows(xt), :] for q in range(r)] + [here]
                    others += [basis[p * RHS + q, z, rows(xt), :] for q in range(r)] + [value]
                    sums = [a + b * value for a, b in zip(sums, others, strict=True)]
                if p < POWERS - 1:
                    packed = pack(packed, value, index)
                    keep_x_faces(p + 1, r, z, xt, value)
        if p < POWERS - 1:
            y_send[p + 1, r] = packed
            send_halos(p + 1, r, slice(2, 6))
        return sums

    def vector(p, r, z, xt):
        return basis[p * RHS + r, z, rows(xt), :]

    def moments(p):
        n = len(PAIRS) * (1 if p == 0 else 2)

        def body(z, sums):
            sums = list(sums)
            for xt in range(xtiles):
                now = [vector(p, r, z, xt) for r in range(RHS)]
                products = []
                if p > 0:
                    before = [vector(p - 1, r, z, xt) for r in range(RHS)]
                    products += [before[r] * now[s] for r, s in PAIRS]
                products += [now[r] * now[s] for r, s in PAIRS]
                sums = [a + b for a, b in zip(sums, products, strict=True)]
            return tuple(sums)

        return list(lax.fori_loop(0, zlen, body, (jnp.zeros((8, 128), F32),) * n))

    def fold(sums, first_group):
        tile = jnp.zeros((8, 128), F32)
        for g in range(0, len(sums), 8):
            some = [jnp.sum(s, axis=0, keepdims=True) for s in sums[g : g + 8]]
            some += [jnp.zeros((1, 128), F32)] * (8 - len(some))
            sums_of = jnp.sum(jnp.concatenate(some, 0), axis=1, keepdims=True)
            tile = jnp.where(lane == 8 * first_group + g + sub, sums_of, tile)
        return jnp.sum(tile, axis=0, keepdims=True)

    relayed = n_gx == 16 and n_gy == 8

    def relay(sem, offsets):
        if relayed:
            for axis, k in offsets:
                pl.semaphore_signal(sem, inc=1, device_id={axis: ring(axis, k)}, device_id_type=MESH)

    near = [(axis, k) for axis in ("gx", "gy") for k in (2, -2)]
    far = [("gx", k) for k in (4, -4)]

    early = []
    for p in range(POWERS - 1):
        step(p, 0)
        if p == 0:
            relay(relay_near, near)
        if p == 1 and relayed:
            pl.semaphore_wait(relay_near, len(near))
            relay(relay_far, far)
        lax.fori_loop(1, RHS, lambda r, c, p=p: (step(p, r), c)[1], 0)
        early += moments(p)
    tile0[...] = fold(early, FIRST_GROUP[0])

    late = []
    for r in range(RHS - 1):
        late += step(POWERS - 1, r)
    tile0[...] += fold(late, FIRST_GROUP[1])
    if relayed:
        pl.semaphore_wait(relay_far, len(far))
    late = step(POWERS - 1, RHS - 1)
    tile0[...] += fold(late, FIRST_GROUP[2])

    def exchange(src, dst, phase, device):
        pltpu.make_async_remote_copy(
            src_ref=src, dst_ref=dst, send_sem=sum_send.at[phase],
            recv_sem=sum_recv.at[phase], device_id=device, device_id_type=MESH,
        ).start()

    def wait_sums(sems, phase, number):
        wait_bytes(count_ref.at[pl.ds(0, number)], sems.at[phase])

    n_plane = n_y * n_gz
    slot = (gy // 2) * n_gz + gz

    exchange(tile0, pair_buf, 0, {"gy": gy + 1 - 2 * lax.rem(gy, 2)})
    wait_sums(sum_recv, 0, 1)
    tile1[...] = tile0[...] + pair_buf[...]

    for k in plane:
        exchange(tile1, plane_buf.at[slot], 1, plane_dev(k))
    plane_buf[slot] = tile1[...]
    for p in range(POWERS):
        wait_bytes(right_hbm.at[:, pl.ds(0, 3)], halo_send.at[p])
    wait_sums(sum_send, 0, 1)
    wait_sums(sum_recv, 1, n_plane - 1)
    tile2[...] = tree_sum([plane_buf[i] for i in range(n_plane)])

    for k in line:
        exchange(tile2, line_buf.at[gx], 2, {"gx": ring("gx", k)})
    line_buf[gx] = tile2[...]
    wait_sums(sum_send, 1, n_plane - 1)
    wait_sums(sum_recv, 2, n_gx - 1)
    total_out[...] = tree_sum([line_buf[i] for i in range(n_gx)])
    wait_sums(sum_send, 2, n_gx - 1)


def factor_kernel(
    total, basis, ortho_hbm, factor_hbm, table, coeff, result, factor, out_sem, factor_sem
):
    width = RHS * POWERS
    zlen, xlen = basis.shape[1], basis.shape[2]
    whole = total[...]
    places = lax.broadcasted_iota(jnp.int32, (8, 128), 1) - lax.broadcasted_iota(
        jnp.int32, (8, 128), 0
    )
    for g in range(GROUPS):
        column = jnp.sum(jnp.where(places == 8 * g, whole, 0.0), axis=1, keepdims=True)
        table[8 * g : 8 * g + 8, :] = jnp.broadcast_to(column, (8, 128))

    def gram(i, j):
        r, s = sorted((i % RHS, j % RHS))
        row = ROW_OF[(i // RHS + j // RHS, (r, s))]
        return jnp.broadcast_to(table[row : row + 1, :], (8, 128))

    lane = lax.broadcasted_iota(jnp.int32, (1, 128), 1)
    upper = {}
    for k in range(width):
        rest = {}
        for j in range(k, width):
            value = gram(k, j)
            for i in range(k):
                value = value - upper[i, k] * upper[i, j]
            rest[j] = value
        pivot = rest[k]
        inverse = lax.rsqrt(pivot)
        inverse = inverse * (1.5 - 0.5 * pivot * inverse * inverse)
        row = jnp.zeros((1, 128), F32)
        for j in range(k, width):
            upper[k, j] = rest[j] * inverse
            row = jnp.where(lane == j, upper[k, j][0:1, :], row)
            coeff[k * width + j] = inverse if j == k else upper[k, j]
        factor[k : k + 1, :] = row[:, :width]
    factor_copy = pltpu.make_async_copy(factor, factor_hbm, factor_sem)
    factor_copy.start()

    def body(z, carry):
        for xt in range(0, xlen // 8, 2):
            cols = [
                [basis[j, z, pl.ds(8 * (xt + h), 8), :] for j in range(width)] for h in range(2)
            ]
            for i in range(width):
                scale = coeff[i * width + i]
                for h in range(2):
                    cols[h][i] = cols[h][i] * scale
                    result[i, z, pl.ds(8 * (xt + h), 8), :] = cols[h][i]
                for j in range(i + 1, width):
                    weight = coeff[i * width + j]
                    for h in range(2):
                        cols[h][j] = cols[h][j] - weight * cols[h][i]
        pltpu.make_async_copy(result.at[:, z], ortho_hbm.at[:, z], out_sem.at[z]).start()
        return carry

    lax.fori_loop(0, zlen, body, 0)
    for z in range(zlen):
        pltpu.make_async_copy(result.at[:, z], ortho_hbm.at[:, z], out_sem.at[z]).wait()
    factor_copy.wait()


def local(sizes, right_side, start_guess, diagonal):
    zlen, xlen, ylen = diagonal.shape
    width = RHS * POWERS
    block = (width, zlen, xlen, ylen)
    any_spec = pl.BlockSpec(memory_space=pl.ANY)
    vmem_spec = pl.BlockSpec(memory_space=pltpu.VMEM)
    n_gx, n_gy, n_gz = sizes
    planes = (n_gy // 2) * n_gz
    face = (POWERS, RHS, 8, 128)
    tile = pltpu.VMEM((1, 128), F32)
    basis, total = pl.pallas_call(
        functools.partial(power_kernel, sizes),
        out_shape=(jax.ShapeDtypeStruct(block, F32), jax.ShapeDtypeStruct((1, 128), F32)),
        in_specs=[any_spec] * 3,
        out_specs=(vmem_spec, vmem_spec),
        scratch_shapes=[
            pltpu.VMEM((RHS, zlen, xlen, ylen), F32),
            pltpu.VMEM((RHS, zlen, xlen, ylen), F32),
            pltpu.VMEM((zlen, xlen, ylen), F32),
            pltpu.VMEM((POWERS, RHS, xlen, ylen), F32),
            pltpu.VMEM((POWERS, RHS, xlen, ylen), F32),
            pltpu.VMEM(face, F32),
            pltpu.VMEM(face, F32),
            pltpu.VMEM(face, F32),
            pltpu.VMEM((POWERS, RHS, 2, 8, 128), F32),
            pltpu.VMEM(face, F32),
            pltpu.VMEM(face, F32),
            tile,
            tile,
            tile,
            tile,
            pltpu.VMEM((planes, 1, 128), F32),
            pltpu.VMEM((n_gx, 1, 128), F32),
            pltpu.VMEM((max(planes, n_gx), 1, 128), F32),
            pltpu.SemaphoreType.DMA((RHS + 2,)),
            pltpu.SemaphoreType.DMA((POWERS,)),
            pltpu.SemaphoreType.DMA((POWERS, RHS)),
            pltpu.SemaphoreType.DMA((3,)),
            pltpu.SemaphoreType.DMA((3,)),
            pltpu.SemaphoreType.REGULAR,
            pltpu.SemaphoreType.REGULAR,
        ],
        compiler_params=pltpu.CompilerParams(
            collective_id=0, has_side_effects=True, vmem_limit_bytes=24 << 20
        ),
    )(*[pltpu.with_memory_space_constraint(x, pltpu.HBM) for x in (right_side, start_guess, diagonal)])
    return pl.pallas_call(
        factor_kernel,
        out_shape=(
            jax.ShapeDtypeStruct(block, F32),
            jax.ShapeDtypeStruct((width, width), F32),
        ),
        in_specs=[vmem_spec, vmem_spec],
        out_specs=(any_spec, any_spec),
        scratch_shapes=[
            pltpu.VMEM((8 * GROUPS, 128), F32),
            pltpu.VMEM((width * width, 8, 128), F32),
            pltpu.VMEM(block, F32),
            pltpu.VMEM((width, width), F32),
            pltpu.SemaphoreType.DMA((zlen,)),
            pltpu.SemaphoreType.DMA,
        ],
        compiler_params=pltpu.CompilerParams(vmem_limit_bytes=24 << 20),
    )(total, basis)


def solution(mesh):
    placed = (P(None, "gz", "gx", "gy"), P(None, "gz", "gx", "gy"), P("gz", "gx", "gy"))
    sizes = tuple(mesh.shape[a] for a in ("gx", "gy", "gz"))
    return jax.shard_map(
        functools.partial(local, sizes),
        mesh=mesh,
        in_specs=placed,
        out_specs=(P(None, "gz", "gx", "gy"), P()),
        check_vma=False,
    )
```

```python
import functools

import jax
import jax.numpy as jnp
from jax import lax
from jax.experimental import pallas as pl
from jax.experimental.pallas import tpu as pltpu
from jax.sharding import PartitionSpec as P

MESH = pl.DeviceIdType.MESH
F32 = jnp.float32
RHS = 4
POWERS = 4
shift_value = 7.125
scale_value = 3.0

PAIRS = [(r, s) for r in range(RHS) for s in range(r, RHS)]
EARLY = [(k, pair) for k in range(5) for pair in PAIRS]
LATE = [[(k, (r, s)) for k in (5, 6) for r in range(s + 1)] for s in range(RHS)]
BATCHES = [EARLY, sum(LATE[:-1], []), LATE[-1]]
FIRST_GROUP = [0]
for entries in BATCHES:
    FIRST_GROUP.append(FIRST_GROUP[-1] - (-len(entries) // 8))
GROUPS = FIRST_GROUP[-1]
ROW_OF = {
    entry: 8 * first + row
    for first, entries in zip(FIRST_GROUP, BATCHES)
    for row, entry in enumerate(entries)
}


def ring(axis, offset):
    count = lax.axis_size(axis)
    return lax.rem(lax.axis_index(axis) + (offset + count), count)


def far_first(offsets, distance):
    return sorted(offsets, key=lambda k: -distance(k))


def tree_sum(values):
    values = list(values)
    while len(values) > 1:
        values = [
            values[i] + values[i + 1] if i + 1 < len(values) else values[i]
            for i in range(0, len(values), 2)
        ]
    return values[0]


def power_kernel(
    sizes, right_hbm, guess_hbm, diag_hbm, basis, total_out,
    guess, right, diag, partial, z_low, z_high, y_send, y_low, y_high, x_send, x_low, x_high,
    tile0, tile1, tile2, pair_buf, plane_buf, line_buf, count_ref,
    in_sem, halo_send, halo_recv, sum_send, sum_recv, relay_near, relay_far,
):
    n_gx, n_gy, n_gz = sizes
    n_y = n_gy // 2
    zlen, xlen = diag.shape[0], diag.shape[1]
    xtiles = xlen // 8
    gx, gy, gz = (lax.axis_index(a) for a in ("gx", "gy", "gz"))

    load_guess = [
        pltpu.make_async_copy(guess_hbm.at[r], guess.at[r], in_sem.at[r]) for r in range(RHS)
    ]
    load_rest = [
        pltpu.make_async_copy(diag_hbm, diag, in_sem.at[RHS]),
        pltpu.make_async_copy(right_hbm, right, in_sem.at[RHS + 1]),
    ]
    load_guess[0].start()

    def dist(k, n):
        return min(k, n - k)

    plane = [(dy, dx) for dy in range(n_y) for dx in range(n_gz) if (dy, dx) != (0, 0)]
    plane = far_first(plane, lambda k: dist(k[0], n_y) + dist(k[1], n_gz))
    line = far_first(range(1, n_gx), lambda k: dist(k, n_gx))

    def plane_dev(k):
        return {"gy": ring("gy", 2 * k[0]), "gz": ring("gz", k[1])}

    barrier = pltpu.get_barrier_semaphore()
    greeted = [{a: ring(a, k)} for a in ("gz", "gx", "gy") for k in (1, -1)]
    for device in greeted:
        pl.semaphore_signal(barrier, inc=1, device_id=device, device_id_type=MESH)

    for copy in load_guess[1:] + load_rest:
        copy.start()

    lane = lax.broadcasted_iota(jnp.int32, (8, 128), 1)
    sub = lax.broadcasted_iota(jnp.int32, (8, 128), 0)
    lane_half = lane // 2
    odd = lane % 2 == 1
    first_lane, last_lane = lane == 0, lane == 127
    first_row, last_row = sub == 0, sub == 7
    y_has = [(gy > 0).astype(F32), (gy < n_gy - 1).astype(F32)]
    x_has = [(gx > 0).astype(F32), (gx < n_gx - 1).astype(F32)]
    z_has = [(gz > 0).astype(F32), (gz < n_gz - 1).astype(F32)]

    def rows(xt):
        return pl.ds(8 * xt, 8)

    def source(p, r):
        return (guess, r) if p == 0 else (basis, (p - 1) * RHS + r)

    def pack(packed, value, index):
        return jnp.where(lane_half == index, pltpu.roll(value, 2 * index + 1, 1), packed)

    def send_halos(p, r, part):
        ref, slot = source(p, r)
        sends = [
            (ref.at[slot, zlen - 1], z_low.at[p, r], {"gz": ring("gz", 1)}),
            (ref.at[slot, 0], z_high.at[p, r], {"gz": ring("gz", -1)}),
            (x_send.at[p, r, 1], x_low.at[p, r], {"gx": ring("gx", 1)}),
            (x_send.at[p, r, 0], x_high.at[p, r], {"gx": ring("gx", -1)}),
            (y_send.at[p, r], y_low.at[p, r], {"gy": ring("gy", 1)}),
            (y_send.at[p, r], y_high.at[p, r], {"gy": ring("gy", -1)}),
        ]
        for src, dst, device in sends[part]:
            pltpu.make_async_remote_copy(
                src_ref=src, dst_ref=dst, send_sem=halo_send.at[p],
                recv_sem=halo_recv.at[p, r], device_id=device, device_id_type=MESH,
            ).start()

    def wait_bytes(like, sem):
        pltpu.make_async_copy(like, like, sem).wait()

    def wait_halos(p, r):
        wait_bytes(right_hbm.at[0, pl.ds(0, 3)], halo_recv.at[p, r])

    def keep_x_faces(p, r, z, xt, value):
        if xt == 0:
            x_send[p, r, 0, z : z + 1, :] = value[0:1, :]
        if xt == xtiles - 1:
            x_send[p, r, 1, z : z + 1, :] = value[7:8, :]

    for r in range(RHS):
        load_guess[r].wait()
        packed = jnp.zeros((8, 128), F32)
        for z in range(zlen):
            for xt in range(xtiles):
                value = guess[r, z, rows(xt), :]
                packed = pack(packed, value, z * xtiles + xt)
                keep_x_faces(0, r, z, xt, value)
        y_send[0, r] = packed
        if r == 0:
            pl.semaphore_wait(barrier, len(greeted))
        send_halos(0, r, slice(0, 6))
    for copy in load_rest:
        copy.wait()

    both_lanes = first_lane | last_lane

    def inside(p, r, carry):
        ref, slot = source(p, r)
        for z in range(zlen):
            for xt in range(xtiles):
                here = ref[slot, z, rows(xt), :]
                if xt == 0:
                    below = jnp.where(first_row, 0.0, pltpu.roll(here, 1, 0))
                else:
                    below = ref[slot, z, pl.ds(8 * xt - 1, 8), :]
                if xt == xtiles - 1:
                    above = jnp.where(last_row, 0.0, pltpu.roll(here, 7, 0))
                else:
                    above = ref[slot, z, pl.ds(8 * xt + 1, 8), :]
                left = jnp.where(first_lane, 0.0, pltpu.roll(here, 1, 1))
                other = jnp.where(last_lane, 0.0, pltpu.roll(here, 127, 1))
                beside = (below + above) + (left + other)
                if z > 0:
                    beside = beside + ref[slot, z - 1, rows(xt), :]
                if z < zlen - 1:
                    beside = beside + ref[slot, z + 1, rows(xt), :]
                weight = diag[z, rows(xt), :]
                if p == 0:
                    value = right[r, z, rows(xt), :] - ((6.0 + weight) * here - beside)
                else:
                    value = ((weight + (6.0 - shift_value)) * here - beside) * (1.0 / scale_value)
                partial[r, z, rows(xt), :] = value
        return carry

    z_ends = (0, zlen - 1)
    x_ends = (0, xtiles - 1)
    order = [(z, xt) for z in z_ends for xt in range(xtiles)]
    order += [(z, xt) for z in range(1, zlen - 1) for xt in x_ends]
    x_done = len(order)
    order += [(z, xt) for z in range(1, zlen - 1) for xt in range(1, xtiles - 1)]

    def step(p, r):
        sums = [jnp.zeros((8, 128), F32)] * (2 * (r + 1) if p == POWERS - 1 else 0)
        sign = 1.0 if p == 0 else -1.0 / scale_value
        wait_halos(p, r)
        edges = jnp.where(
            odd,
            pltpu.roll(y_high[p, r] * (y_has[1] * sign), 126, 1),
            y_low[p, r] * (y_has[0] * sign),
        )
        x_lo = x_low[p, r] * (x_has[0] * sign)
        x_hi = x_high[p, r] * (x_has[1] * sign)
        packed = jnp.zeros((8, 128), F32)
        for count, (z, xt) in enumerate(order):
            index = z * xtiles + xt
            edge = edges if index == 0 else pltpu.roll(edges, 128 - 2 * index, 1)
            value = partial[r, z, rows(xt), :] + jnp.where(both_lanes, edge, 0.0)
            if z == 0:
                value = value + z_low[p, r, rows(xt), :] * (z_has[0] * sign)
            if z == zlen - 1:
                value = value + z_high[p, r, rows(xt), :] * (z_has[1] * sign)
            if xt == 0:
                value = value + jnp.where(first_row, x_lo[z : z + 1, :], 0.0)
            if xt == xtiles - 1:
                value = value + jnp.where(last_row, x_hi[z : z + 1, :], 0.0)
            basis[p * RHS + r, z, rows(xt), :] = value
            if p == POWERS - 1:
                others = [basis[(p - 1) * RHS + q, z, rows(xt), :] for q in range(r + 1)]
                others += [basis[p * RHS + q, z, rows(xt), :] for q in range(r)] + [value]
                sums = [a + b * value for a, b in zip(sums, others, strict=True)]
            else:
                packed = pack(packed, value, index)
                keep_x_faces(p + 1, r, z, xt, value)
                if count + 1 == 2 * xtiles:
                    send_halos(p + 1, r, slice(0, 2))
                if count + 1 == x_done:
                    send_halos(p + 1, r, slice(2, 4))
        if p < POWERS - 1:
            y_send[p + 1, r] = packed
            send_halos(p + 1, r, slice(4, 6))
        return sums

    def vector(p, r, z, xt):
        return basis[p * RHS + r, z, rows(xt), :]

    def moments(p):
        n = len(PAIRS) * (1 if p == 0 else 2)

        def body(z, sums):
            sums = list(sums)
            for xt in range(xtiles):
                now = [vector(p, r, z, xt) for r in range(RHS)]
                products = []
                if p > 0:
                    before = [vector(p - 1, r, z, xt) for r in range(RHS)]
                    products += [before[r] * now[s] for r, s in PAIRS]
                products += [now[r] * now[s] for r, s in PAIRS]
                sums = [a + b for a, b in zip(sums, products, strict=True)]
            return tuple(sums)

        return list(lax.fori_loop(0, zlen, body, (jnp.zeros((8, 128), F32),) * n))

    def fold(sums, first_group):
        tile = jnp.zeros((8, 128), F32)
        for g in range(0, len(sums), 8):
            some = [jnp.sum(s, axis=0, keepdims=True) for s in sums[g : g + 8]]
            some += [jnp.zeros((1, 128), F32)] * (8 - len(some))
            sums_of = jnp.sum(jnp.concatenate(some, 0), axis=1, keepdims=True)
            tile = jnp.where(lane == 8 * first_group + g + sub, sums_of, tile)
        return jnp.sum(tile, axis=0, keepdims=True)

    relayed = n_gx == 16 and n_gy == 8

    def relay(sem, offsets):
        if relayed:
            for axis, k in offsets:
                pl.semaphore_signal(sem, inc=1, device_id={axis: ring(axis, k)}, device_id_type=MESH)

    near = [(axis, k) for axis in ("gx", "gy") for k in (2, -2)]
    far = [("gx", k) for k in (4, -4)]

    early = []
    for p in range(POWERS - 1):
        lax.fori_loop(0, RHS, functools.partial(inside, p), 0)
        if p > 0:
            early += moments(p - 1)
        step(p, 0)
        if p == 0:
            relay(relay_near, near)
        if p == 1 and relayed:
            pl.semaphore_wait(relay_near, len(near))
            relay(relay_far, far)
        lax.fori_loop(1, RHS, lambda r, c, p=p: (step(p, r), c)[1], 0)
    lax.fori_loop(0, RHS, functools.partial(inside, POWERS - 1), 0)
    early += moments(POWERS - 2)
    tile0[...] = fold(early, FIRST_GROUP[0])

    late = []
    for r in range(RHS - 1):
        late += step(POWERS - 1, r)
    tile0[...] += fold(late, FIRST_GROUP[1])
    if relayed:
        pl.semaphore_wait(relay_far, len(far))
    late = step(POWERS - 1, RHS - 1)
    tile0[...] += fold(late, FIRST_GROUP[2])

    def exchange(src, dst, phase, device):
        pltpu.make_async_remote_copy(
            src_ref=src, dst_ref=dst, send_sem=sum_send.at[phase],
            recv_sem=sum_recv.at[phase], device_id=device, device_id_type=MESH,
        ).start()

    def wait_sums(sems, phase, number):
        wait_bytes(count_ref.at[pl.ds(0, number)], sems.at[phase])

    n_plane = n_y * n_gz
    slot = (gy // 2) * n_gz + gz

    exchange(tile0, pair_buf, 0, {"gy": gy + 1 - 2 * lax.rem(gy, 2)})
    wait_sums(sum_recv, 0, 1)
    tile1[...] = tile0[...] + pair_buf[...]

    for k in plane:
        exchange(tile1, plane_buf.at[slot], 1, plane_dev(k))
    plane_buf[slot] = tile1[...]
    for p in range(POWERS):
        wait_bytes(right_hbm.at[:, pl.ds(0, 3)], halo_send.at[p])
    wait_sums(sum_send, 0, 1)
    wait_sums(sum_recv, 1, n_plane - 1)
    tile2[...] = tree_sum([plane_buf[i] for i in range(n_plane)])

    for k in line:
        exchange(tile2, line_buf.at[gx], 2, {"gx": ring("gx", k)})
    line_buf[gx] = tile2[...]
    wait_sums(sum_send, 1, n_plane - 1)
    wait_sums(sum_recv, 2, n_gx - 1)
    total_out[...] = tree_sum([line_buf[i] for i in range(n_gx)])
    wait_sums(sum_send, 2, n_gx - 1)


def factor_kernel(
    total, basis, ortho_hbm, factor_hbm, table, coeff, result, factor, out_sem, factor_sem
):
    width = RHS * POWERS
    zlen, xlen = basis.shape[1], basis.shape[2]
    whole = total[...]
    places = lax.broadcasted_iota(jnp.int32, (8, 128), 1) - lax.broadcasted_iota(
        jnp.int32, (8, 128), 0
    )
    for g in range(GROUPS):
        column = jnp.sum(jnp.where(places == 8 * g, whole, 0.0), axis=1, keepdims=True)
        table[8 * g : 8 * g + 8, :] = jnp.broadcast_to(column, (8, 128))

    def gram(i, j):
        r, s = sorted((i % RHS, j % RHS))
        row = ROW_OF[(i // RHS + j // RHS, (r, s))]
        return jnp.broadcast_to(table[row : row + 1, :], (8, 128))

    lane = lax.broadcasted_iota(jnp.int32, (1, 128), 1)
    upper = {}
    for k in range(width):
        rest = {}
        for j in range(k, width):
            value = gram(k, j)
            for i in range(k):
                value = value - upper[i, k] * upper[i, j]
            rest[j] = value
        pivot = rest[k]
        inverse = lax.rsqrt(pivot)
        inverse = inverse * (1.5 - 0.5 * pivot * inverse * inverse)
        row = jnp.zeros((1, 128), F32)
        for j in range(k, width):
            upper[k, j] = rest[j] * inverse
            row = jnp.where(lane == j, upper[k, j][0:1, :], row)
            coeff[k * width + j] = inverse if j == k else upper[k, j]
        factor[k : k + 1, :] = row[:, :width]
    factor_copy = pltpu.make_async_copy(factor, factor_hbm, factor_sem)
    factor_copy.start()

    def body(z, carry):
        for xt in range(0, xlen // 8, 2):
            cols = [
                [basis[j, z, pl.ds(8 * (xt + h), 8), :] for j in range(width)] for h in range(2)
            ]
            for i in range(width):
                scale = coeff[i * width + i]
                for h in range(2):
                    cols[h][i] = cols[h][i] * scale
                    result[i, z, pl.ds(8 * (xt + h), 8), :] = cols[h][i]
                for j in range(i + 1, width):
                    weight = coeff[i * width + j]
                    for h in range(2):
                        cols[h][j] = cols[h][j] - weight * cols[h][i]
        pltpu.make_async_copy(result.at[:, z], ortho_hbm.at[:, z], out_sem.at[z]).start()
        return carry

    lax.fori_loop(0, zlen, body, 0)
    for z in range(zlen):
        pltpu.make_async_copy(result.at[:, z], ortho_hbm.at[:, z], out_sem.at[z]).wait()
    factor_copy.wait()


def local(sizes, right_side, start_guess, diagonal):
    zlen, xlen, ylen = diagonal.shape
    width = RHS * POWERS
    block = (width, zlen, xlen, ylen)
    any_spec = pl.BlockSpec(memory_space=pl.ANY)
    vmem_spec = pl.BlockSpec(memory_space=pltpu.VMEM)
    n_gx, n_gy, n_gz = sizes
    planes = (n_gy // 2) * n_gz
    face = (POWERS, RHS, 8, 128)
    tile = pltpu.VMEM((1, 128), F32)
    basis, total = pl.pallas_call(
        functools.partial(power_kernel, sizes),
        out_shape=(jax.ShapeDtypeStruct(block, F32), jax.ShapeDtypeStruct((1, 128), F32)),
        in_specs=[any_spec] * 3,
        out_specs=(vmem_spec, vmem_spec),
        scratch_shapes=[
            pltpu.VMEM((RHS, zlen, xlen, ylen), F32),
            pltpu.VMEM((RHS, zlen, xlen, ylen), F32),
            pltpu.VMEM((zlen, xlen, ylen), F32),
            pltpu.VMEM((RHS, zlen, xlen, ylen), F32),
            pltpu.VMEM((POWERS, RHS, xlen, ylen), F32),
            pltpu.VMEM((POWERS, RHS, xlen, ylen), F32),
            pltpu.VMEM(face, F32),
            pltpu.VMEM(face, F32),
            pltpu.VMEM(face, F32),
            pltpu.VMEM((POWERS, RHS, 2, 8, 128), F32),
            pltpu.VMEM(face, F32),
            pltpu.VMEM(face, F32),
            tile,
            tile,
            tile,
            tile,
            pltpu.VMEM((planes, 1, 128), F32),
            pltpu.VMEM((n_gx, 1, 128), F32),
            pltpu.VMEM((max(planes, n_gx), 1, 128), F32),
            pltpu.SemaphoreType.DMA((RHS + 2,)),
            pltpu.SemaphoreType.DMA((POWERS,)),
            pltpu.SemaphoreType.DMA((POWERS, RHS)),
            pltpu.SemaphoreType.DMA((3,)),
            pltpu.SemaphoreType.DMA((3,)),
            pltpu.SemaphoreType.REGULAR,
            pltpu.SemaphoreType.REGULAR,
        ],
        compiler_params=pltpu.CompilerParams(
            collective_id=0, has_side_effects=True, vmem_limit_bytes=24 << 20
        ),
    )(*[pltpu.with_memory_space_constraint(x, pltpu.HBM) for x in (right_side, start_guess, diagonal)])
    return pl.pallas_call(
        factor_kernel,
        out_shape=(
            jax.ShapeDtypeStruct(block, F32),
            jax.ShapeDtypeStruct((width, width), F32),
        ),
        in_specs=[vmem_spec, vmem_spec],
        out_specs=(any_spec, any_spec),
        scratch_shapes=[
            pltpu.VMEM((8 * GROUPS, 128), F32),
            pltpu.VMEM((width * width, 8, 128), F32),
            pltpu.VMEM(block, F32),
            pltpu.VMEM((width, width), F32),
            pltpu.SemaphoreType.DMA((zlen,)),
            pltpu.SemaphoreType.DMA,
        ],
        compiler_params=pltpu.CompilerParams(vmem_limit_bytes=24 << 20),
    )(total, basis)


def solution(mesh):
    placed = (P(None, "gz", "gx", "gy"), P(None, "gz", "gx", "gy"), P("gz", "gx", "gy"))
    sizes = tuple(mesh.shape[a] for a in ("gx", "gy", "gz"))
    return jax.shard_map(
        functools.partial(local, sizes),
        mesh=mesh,
        in_specs=placed,
        out_specs=(P(None, "gz", "gx", "gy"), P()),
        check_vma=False,
    )
```
